32 devices in a mesh: group: 4 (over y, core), shard: 8 (over z, x).
Axes of the slice: x: 2, y: 2, z: 4, core: 2. Of those that a mesh axis runs over, the one named last changes fastest.
Arguments:
- embeddings: bfloat16 [16384, 1024], P(('group', 'shard')), may hold values from -30 to 30
- destinations: int32 [2048, 1], P(('group', 'shard')), may hold values from 0 to 7; in each aligned block of 64 rows (0 to 63, 64 to 127, ...) at most 12 rows name the same one
- means: float32 [1024], replicated, may hold values from -0.5 to 0.5
- scales: float32 [1024], replicated, may hold values from 0.01 to 0.1
Outputs:
- codes: int32 [24576, 128], P(('group', 'shard'))
- quantized: bfloat16 [24576, 1024], P(('group', 'shard'))
- statistics: float32 [2, 1024], replicated
The draws below stay inside these ranges and needn't reach their ends.
Inputs may be any that keep to these rules, and one draw needn't show every extreme that they name: `destinations`: within the 64 blocks of one device, no owner is named by more than 12 blocks.
All inputs are finite; a program needn't handle non-finite values.
Results may differ from the reference program's by a relative error of at most 0.0015.
Values may be sent and summed in bfloat16 or wider, within the bound.
A program may use at most 64 MiB of HBM per device.

```python
import math
import jax
import jax.numpy as jnp
import numpy as np
from jax import lax

D = 1024
BLOCK_ROWS = 8
BLK_DEV = 64
PEER_CAP = 12
BLOCKS = 2048
ROWS = 16384
N_GROUP = 4
N_SHARD = 8


def draw_embeddings(key, part):
    first = jax.random.fold_in(jax.random.fold_in(key, 11), 0)
    ramp = 1.0 + 2.0 * jnp.arange(ROWS, dtype=jnp.float32) / ROWS
    values = jax.random.normal(first, (ROWS, D), jnp.float32) * ramp[:, None]
    return jnp.clip(values, -30.0, 30.0).astype(jnp.bfloat16)


def deal_out(key, own, number, rows, amount, top, reach, slope):
    ranking = jax.random.permutation(key, amount)
    crowded, usual = shares(amount, rows * top, reach, slope, True), shares(amount, rows * top, reach, slope, False)
    places = jnp.arange(amount)

    def named(tallies, offset_by):
        used = int((tallies > 0).sum())
        fixed = max(1, used // 4)
        moved = fixed + (places - fixed + offset_by * (used - fixed)) % max(1, amount - fixed)
        return jnp.zeros((amount,), jnp.int32).at[ranking[jnp.where(places < fixed, places, moved)]].set(jnp.asarray(tallies, jnp.int32))

    tallies = jnp.where(number % 4 == 0, named(crowded, number // 4), named(usual, number - number // 4 - 1))
    mixed = jax.random.permutation(jax.random.fold_in(own, 3), amount)
    donor, receiver = mixed[0:amount // 2 * 2:2], mixed[1:amount // 2 * 2:2]
    room = jnp.minimum(tallies[donor] - 1, reach - tallies[receiver]) // 2
    room = jnp.where((donor == ranking[0]) | (receiver == ranking[0]) | (tallies[receiver] == 0), 0, jnp.maximum(room, 0))
    moved = jax.random.randint(jax.random.fold_in(own, 4), (amount // 2,), 0, 1 << 20) % (room + 1)
    tallies = tallies.at[donor].add(-moved).at[receiver].add(moved)
    items = jnp.searchsorted(jnp.cumsum(tallies), jnp.arange(rows * top), side="right").astype(jnp.int32)
    grid = items.reshape(top, rows).T
    grid = grid[jax.random.permutation(jax.random.fold_in(own, 1), rows)]
    offset_by = jax.random.randint(jax.random.fold_in(own, 2), (rows, 1), 0, top)
    return jnp.take_along_axis(grid, (jnp.arange(top)[None, :] + offset_by) % top, axis=1)


def shares(number_of, total, limit, skew, full):
    weights = [(1 << 20) // math.isqrt(rank ** skew) + 1 for rank in range(1, number_of + 1)]
    largest = limit if full else min(limit, max(-(-total // number_of), total * weights[0] // sum(weights)))
    least = 1 if total - largest >= number_of - 1 else 0
    counts, rest = [largest] + [least] * (number_of - 1), total - largest - least * (number_of - 1)
    while rest > 0:
        movable = [i for i in range(1, number_of) if counts[i] < largest] or [i for i in range(1, number_of) if counts[i] < limit]
        whole, budget = sum([weights[i] for i in movable]), rest
        for i in movable:
            addition = min(limit - counts[i], max(1, budget * weights[i] // whole), rest)
            counts[i] = counts[i] + addition
            rest = rest - addition
    return np.array(counts)


def setup_inputs(seed: int = 0) -> dict:
    seeds = jax.random.split(jax.random.key(seed), 5)
    embeddings = draw_embeddings(jax.random.fold_in(seeds[4], 71), 0)
    destinations_keys = jax.random.split(jax.random.fold_in(seeds[1], 1), BLOCKS // BLK_DEV)
    destinations_turns = jax.random.permutation(jax.random.fold_in(seeds[1], 3), BLOCKS // BLK_DEV)
    destinations = jax.vmap(lambda own, number: deal_out(jax.random.fold_in(seeds[1], 2), own, number, BLK_DEV, N_SHARD, 1, PEER_CAP, 2))(destinations_keys, destinations_turns).reshape((BLOCKS, 1))
    means = jnp.clip(jax.random.uniform(seeds[2], (D,), jnp.float32, -0.5, 0.5), -0.5, 0.5)
    scales = jnp.clip(jnp.exp(jax.random.uniform(seeds[3], (D,), jnp.float32, math.log(0.01), math.log(0.1))), 0.01, 0.1)
    return dict(embeddings=embeddings, destinations=destinations, means=means, scales=scales)


def encode(rows, live, means, scales):
    centered = rows.astype(jnp.float32) - means
    bits = (centered > 0).astype(jnp.int32)
    bits = bits.reshape(rows.shape[:-1] + (rows.shape[-1] // 8, 8))
    weights = jnp.left_shift(jnp.int32(1), jnp.arange(8, dtype=jnp.int32))
    codes = jnp.sum(bits * weights, axis=-1) * live[..., None]
    quant = jnp.clip(centered / scales, -127.0, 127.0) * live[..., None].astype(jnp.float32)
    return codes.astype(jnp.int32), quant.astype(jnp.bfloat16)


def one_group(operands, means, scales):
    blocks_in, owners = operands
    sources = owners.shape[0]
    same = owners[:, :, None] == owners[:, None, :]
    order = jnp.arange(BLK_DEV, dtype=jnp.int32)
    earlier = order[None, :] < order[:, None]
    slot = jnp.sum((same & earlier[None]).astype(jnp.int32), axis=-1).astype(jnp.int32)
    source_ids = jnp.broadcast_to(jnp.arange(sources, dtype=jnp.int32)[:, None], owners.shape)
    buffer = jnp.zeros((sources, sources, PEER_CAP, BLOCK_ROWS, D), jnp.bfloat16)
    buffer = buffer.at[owners, source_ids, slot].set(blocks_in)
    live = jnp.zeros((sources, sources, PEER_CAP), jnp.int32).at[owners, source_ids, slot].set(1)
    live_rows = jnp.broadcast_to(live[..., None], (sources, sources, PEER_CAP, BLOCK_ROWS))
    codes, quant = encode(buffer, live_rows, means, scales)
    return codes.reshape(-1, D // 8), quant.reshape(-1, D)


def reference(embeddings, destinations, means, scales):
    blocks_in = embeddings.reshape(N_GROUP, N_SHARD, BLK_DEV, BLOCK_ROWS, D)
    owners = destinations.reshape(N_GROUP, N_SHARD, BLK_DEV).astype(jnp.int32)
    codes, quant = lax.map(lambda operands: one_group(operands, means, scales), (blocks_in, owners))
    sums = jnp.sum(embeddings, axis=0, dtype=jnp.float32)
    squares = jnp.sum(jnp.square(embeddings.astype(jnp.float32)), axis=0)
    return codes.reshape(-1, D // 8), quant.reshape(-1, D), jnp.stack([sums, squares])
```

```python
import functools

import jax
import jax.numpy as jnp
from jax import lax
from jax.experimental import pallas as pl
from jax.experimental.pallas import tpu as pltpu
from jax.sharding import PartitionSpec as P

BLOCK_ROWS = 8
ABSENT = 1024.0
BOUND = 64.0
MESH = pl.DeviceIdType.MESH


def kernel(
    n, groups, cap,
    emb_hbm, dest_ref, means_ref, scales_ref,
    codes_hbm, quant_hbm, stats_ref,
    emb, placed, arrived, codes, quant, weights, by_group, by_shard,
    in_sem, send_sems, recv_sems, gsend_sems, grecv_sems, ssend_sems, srecv_sems,
    codes_sems, quant_sems,
):
    g, me = lax.axis_index("group"), lax.axis_index("shard")
    rows_in, width = emb.shape
    blocks = rows_in // BLOCK_ROWS
    rows = cap * BLOCK_ROWS
    half = n // 2
    side = me // half

    load = pltpu.make_async_copy(emb_hbm, emb, in_sem)
    load.start()
    barrier = pltpu.get_barrier_semaphore()

    @pl.loop(1, n)
    def _(k):
        pl.semaphore_signal(barrier, 1, device_id=(g, lax.rem(me + k, n)), device_id_type=MESH)

    @pl.loop(1, groups)
    def _(k):
        pl.semaphore_signal(barrier, 1, device_id=(lax.rem(g + k, groups), me), device_id_type=MESH)

    owner = dest_ref[...]
    block = lax.broadcasted_iota(jnp.int32, (blocks, rows_in), 0)
    column = lax.broadcasted_iota(jnp.int32, (blocks, rows_in), 1)
    column_block = lax.shift_right_logical(column, BLOCK_ROWS.bit_length() - 1)
    owner_wide = jnp.broadcast_to(owner, (blocks, rows_in))
    owner_row = jnp.sum(jnp.where(block == column_block, owner_wide, 0), axis=0, keepdims=True)
    before = (owner_wide == owner_row) & (block < column_block)
    slot_row = jnp.sum(before.astype(jnp.int32), axis=0, keepdims=True)
    target_row = (owner_row * cap + slot_row) * BLOCK_ROWS + (column[:1] & (BLOCK_ROWS - 1))
    place = lax.broadcasted_iota(jnp.int32, (rows, rows_in), 0)
    place_row = lax.broadcasted_iota(jnp.int32, (rows, width), 0)

    def arrange(peer, out, at):
        picks = (target_row - peer * rows == place).astype(jnp.float32).astype(jnp.bfloat16)
        count = jnp.sum((owner == peer).astype(jnp.int32), axis=0, keepdims=True)
        moved = jnp.dot(picks, emb[...], preferred_element_type=jnp.float32)
        filled = place_row < jnp.broadcast_to(count * BLOCK_ROWS, (rows, width))
        out[at] = jnp.where(filled, moved, ABSENT).astype(jnp.bfloat16)

    def across(k):
        return (1 - side) * half + lax.rem(me + k, half)

    def beside(k):
        return side * half + lax.rem(me + k, half)

    def send(peer):
        return pltpu.make_async_remote_copy(
            src_ref=placed.at[peer], dst_ref=arrived.at[me],
            send_sem=send_sems.at[peer], recv_sem=recv_sems.at[me],
            device_id=(g, peer), device_id_type=MESH,
        )

    def receive(peer):
        return pltpu.make_async_remote_copy(
            src_ref=placed.at[peer], dst_ref=arrived.at[peer],
            send_sem=send_sems.at[peer], recv_sem=recv_sems.at[peer],
            device_id=(g, peer), device_id_type=MESH,
        )

    load.wait()
    first = across(0)
    arrange(first, placed, first)
    pl.semaphore_wait(barrier, n - 1 + groups - 1)
    send(first).start()

    @pl.loop(1, half)
    def _(k):
        arrange(across(k), placed, across(k))
        send(across(k)).start()

    @pl.loop(1, half)
    def _(k):
        arrange(beside(k), placed, beside(k))
        send(beside(k)).start()

    tile = 64
    total = jnp.zeros((8, width), jnp.float32)
    square = jnp.zeros((8, width), jnp.float32)

    def add(i, carry):
        total, square = carry
        x = emb[pl.ds(pl.multiple_of(i * tile, tile), tile), :].astype(jnp.float32)
        x = x.reshape(tile // 8, 8, width)
        return total + jnp.sum(x, axis=0), square + jnp.sum(x * x, axis=0)

    total, square = lax.fori_loop(0, rows_in // tile, add, (total, square))
    by_group[g, 0:1, :] = jnp.sum(total, axis=0, keepdims=True)
    by_group[g, 1:2, :] = jnp.sum(square, axis=0, keepdims=True)

    def to_group(peer, slot):
        return pltpu.make_async_remote_copy(
            src_ref=by_group.at[g], dst_ref=by_group.at[slot],
            send_sem=gsend_sems.at[peer], recv_sem=grecv_sems.at[slot],
            device_id=(peer, me), device_id_type=MESH,
        )

    def to_shard(peer, slot):
        return pltpu.make_async_remote_copy(
            src_ref=by_shard.at[me], dst_ref=by_shard.at[slot],
            send_sem=ssend_sems.at[peer], recv_sem=srecv_sems.at[slot],
            device_id=(g, peer), device_id_type=MESH,
        )

    @pl.loop(1, groups)
    def _(k):
        to_group(lax.rem(g + k, groups), g).start()

    index = lax.broadcasted_iota(jnp.int32, (width, width // 8), 0)
    byte = lax.broadcasted_iota(jnp.int32, (width, width // 8), 1)
    power = lax.shift_left(jnp.ones_like(index), index & 7)
    weights[...] = jnp.where(lax.shift_right_logical(index, 3) == byte, power, 0).astype(
        jnp.float32).astype(jnp.bfloat16)
    means = means_ref[...]
    inverse = 1.0 / scales_ref[...]
    step = 32 if rows % 32 == 0 else 16

    def write(source):
        at = pl.ds(pl.multiple_of(source * rows, rows), rows)
        return (
            pltpu.make_async_copy(codes.at[source], codes_hbm.at[at], codes_sems.at[source]),
            pltpu.make_async_copy(quant.at[source], quant_hbm.at[at], quant_sems.at[source]),
        )

    def encode(source):
        for r in range(0, rows, step):
            x = arrived[source, r:r + step, :].astype(jnp.float32)
            live = x < BOUND
            centered = x - means
            bits = jnp.where(live & (centered > 0), 1.0, 0.0).astype(jnp.bfloat16)
            scaled = jnp.clip(centered * inverse, -127.0, 127.0)
            quant[source, r:r + step, :] = jnp.where(live, scaled, 0.0).astype(jnp.bfloat16)
            packed = jnp.dot(bits, weights[...], preferred_element_type=jnp.float32)
            codes[source, r:r + step, :] = packed.astype(jnp.int32)
        for copy in write(source):
            copy.start()

    arrange(me, arrived, me)
    encode(me)

    @pl.loop(1, groups)
    def _(k):
        peer = lax.rem(g + k, groups)
        to_group(peer, peer).wait_recv()

    by_shard[me] = jnp.sum(by_group[...], axis=0)

    @pl.loop(1, n)
    def _(k):
        to_shard(lax.rem(me + k, n), me).start()

    @pl.loop(1, half)
    def _(k):
        receive(beside(k)).wait_recv()
        encode(beside(k))

    @pl.loop(1, n)
    def _(k):
        peer = lax.rem(me + k, n)
        to_shard(peer, peer).wait_recv()

    stats_ref[...] = jnp.sum(by_shard[...], axis=0)

    @pl.loop(0, half)
    def _(k):
        receive(across(k)).wait_recv()
        encode(across(k))

    @pl.loop(1, groups)
    def _(k):
        peer = lax.rem(g + k, groups)
        to_group(peer, g).wait_send()

    @pl.loop(1, n)
    def _(k):
        peer = lax.rem(me + k, n)
        send(peer).wait_send()
        to_shard(peer, me).wait_send()

    @pl.loop(0, n)
    def _(k):
        for copy in write(k):
            copy.wait()


def body(n, groups, embeddings, destinations, means, scales):
    rows_in, width = embeddings.shape
    blocks = rows_in // BLOCK_ROWS
    cap = max(2, 3 * blocks // (2 * n))
    rows = cap * BLOCK_ROWS
    hbm = pl.BlockSpec(memory_space=pl.ANY)
    vmem = pl.BlockSpec(memory_space=pltpu.VMEM)
    dma = pltpu.SemaphoreType.DMA
    return pl.pallas_call(
        functools.partial(kernel, n, groups, cap),
        out_shape=(
            jax.ShapeDtypeStruct((n * rows, width // 8), jnp.int32),
            jax.ShapeDtypeStruct((n * rows, width), jnp.bfloat16),
            jax.ShapeDtypeStruct((2, width), jnp.float32),
        ),
        in_specs=[hbm, vmem, vmem, vmem],
        out_specs=(hbm, hbm, vmem),
        scratch_shapes=[
            pltpu.VMEM((rows_in, width), jnp.bfloat16),
            pltpu.VMEM((n, rows, width), jnp.bfloat16),
            pltpu.VMEM((n, rows, width), jnp.bfloat16),
            pltpu.VMEM((n, rows, width // 8), jnp.int32),
            pltpu.VMEM((n, rows, width), jnp.bfloat16),
            pltpu.VMEM((width, width // 8), jnp.bfloat16),
            pltpu.VMEM((groups, 2, width), jnp.float32),
            pltpu.VMEM((n, 2, width), jnp.float32),
            dma(()),
            dma((n,)), dma((n,)),
            dma((groups,)), dma((groups,)),
            dma((n,)), dma((n,)),
            dma((n,)), dma((n,)),
        ],
        compiler_params=pltpu.CompilerParams(
            collective_id=0, has_side_effects=True, vmem_limit_bytes=40 * 2**20
        ),
    )(embeddings, destinations, means.reshape(1, width), scales.reshape(1, width))


def solution(mesh):
    n, groups = mesh.shape["shard"], mesh.shape["group"]
    in_specs = (P(("group", "shard"), None), P(("group", "shard"), None), P(), P())
    out_specs = (P(("group", "shard"), None), P(("group", "shard"), None), P())
    return jax.shard_map(
        functools.partial(body, n, groups),
        mesh=mesh, in_specs=in_specs, out_specs=out_specs, check_vma=False,
    )
```

```python
import functools

import jax
import jax.numpy as jnp
from jax import lax
from jax.experimental import pallas as pl
from jax.experimental.pallas import tpu as pltpu
from jax.sharding import PartitionSpec as P

BLOCK_ROWS = 8
ABSENT = 1024.0
BOUND = 64.0
MESH = pl.DeviceIdType.MESH


def kernel(
    n, groups, cap,
    emb_hbm, dest_hbm, means_hbm, scales_hbm,
    codes_hbm, quant_hbm, stats_hbm,
    emb, dest_ref, means_ref, scales_ref, placed, arrived, codes, quant, weights,
    local, by_group, by_shard, whole, stats_ref,
    in_sems, send_sems, recv_sems, gsend_sems, grecv_sems, ssend_sems, srecv_sems,
    wsend_sems, wrecv_sems, codes_sems, quant_sems, stats_sem,
):
    g, me = lax.axis_index("group"), lax.axis_index("shard")
    rows_in, width = emb.shape
    blocks = rows_in // BLOCK_ROWS
    rows = cap * BLOCK_ROWS
    half = n // 2
    side = me // half

    loads = [
        pltpu.make_async_copy(source, target, in_sems.at[i])
        for i, (source, target) in enumerate(
            ((dest_hbm, dest_ref), (emb_hbm, emb), (means_hbm, means_ref), (scales_hbm, scales_ref))
        )
    ]
    for load in loads:
        load.start()
    barrier = pltpu.get_barrier_semaphore()

    @pl.loop(1, n)
    def _(k):
        pl.semaphore_signal(barrier, 1, device_id=(g, lax.rem(me + k, n)), device_id_type=MESH)

    @pl.loop(1, groups)
    def _(k):
        pl.semaphore_signal(barrier, 1, device_id=(lax.rem(g + k, groups), me), device_id_type=MESH)

    loads[0].wait()
    square_block = lax.broadcasted_iota(jnp.int32, (blocks, blocks), 0)
    square_column = lax.broadcasted_iota(jnp.int32, (blocks, blocks), 1)
    owner_lanes = jnp.broadcast_to(dest_ref[...], (blocks, blocks))
    owner = jnp.sum(
        jnp.where(square_block == square_column, owner_lanes, 0), axis=1, keepdims=True
    )
    block = lax.broadcasted_iota(jnp.int32, (blocks, rows_in), 0)
    column = lax.broadcasted_iota(jnp.int32, (blocks, rows_in), 1)
    column_block = lax.shift_right_logical(column, BLOCK_ROWS.bit_length() - 1)
    owner_wide = jnp.broadcast_to(owner, (blocks, rows_in))
    owner_row = jnp.sum(jnp.where(block == column_block, owner_wide, 0), axis=0, keepdims=True)
    before = (owner_wide == owner_row) & (block < column_block)
    slot_row = jnp.sum(before.astype(jnp.int32), axis=0, keepdims=True)
    target_row = (owner_row * cap + slot_row) * BLOCK_ROWS + (column[:1] & (BLOCK_ROWS - 1))
    place = lax.broadcasted_iota(jnp.int32, (rows, rows_in), 0)
    place_row = lax.broadcasted_iota(jnp.int32, (rows, width), 0)

    def arrange(peer, out, at):
        picks = (target_row - peer * rows == place).astype(jnp.float32).astype(jnp.bfloat16)
        count = jnp.sum((owner == peer).astype(jnp.int32), axis=0, keepdims=True)
        moved = jnp.dot(picks, emb[...], preferred_element_type=jnp.float32)
        filled = place_row < jnp.broadcast_to(count * BLOCK_ROWS, (rows, width))
        out[at] = jnp.where(filled, moved, ABSENT).astype(jnp.bfloat16)

    def across(k):
        return (1 - side) * half + (lax.rem(me, half) ^ k if half & (half - 1) == 0 else lax.rem(me + k, half))

    def beside(k):
        return side * half + lax.rem(me + k, half)

    def send(peer):
        return pltpu.make_async_remote_copy(
            src_ref=placed.at[peer], dst_ref=arrived.at[me],
            send_sem=send_sems.at[peer], recv_sem=recv_sems.at[me],
            device_id=(g, peer), device_id_type=MESH,
        )

    def receive(peer):
        return pltpu.make_async_remote_copy(
            src_ref=placed.at[peer], dst_ref=arrived.at[peer],
            send_sem=send_sems.at[peer], recv_sem=recv_sems.at[peer],
            device_id=(g, peer), device_id_type=MESH,
        )

    loads[1].wait()
    first = across(0)
    arrange(first, placed, first)
    tile = 64
    total = jnp.zeros((8, width), jnp.float32)
    square = jnp.zeros((8, width), jnp.float32)

    def add(i, carry):
        total, square = carry
        x = emb[pl.ds(pl.multiple_of(i * tile, tile), tile), :].astype(jnp.float32)
        x = x.reshape(tile // 8, 8, width)
        return total + jnp.sum(x, axis=0), square + jnp.sum(x * x, axis=0)

    total, square = lax.fori_loop(0, rows_in // tile, add, (total, square))
    part = width // groups
    total = jnp.sum(total, axis=0, keepdims=True)
    square = jnp.sum(square, axis=0, keepdims=True)
    for q in range(groups):
        local[q, 0:1, :] = total[:, q * part:(q + 1) * part]
        local[q, 1:2, :] = square[:, q * part:(q + 1) * part]

    def to_group(peer, slot):
        return pltpu.make_async_remote_copy(
            src_ref=local.at[peer], dst_ref=by_group.at[slot],
            send_sem=gsend_sems.at[peer], recv_sem=grecv_sems.at[slot],
            device_id=(peer, me), device_id_type=MESH,
        )

    def to_shard(peer, slot):
        return pltpu.make_async_remote_copy(
            src_ref=by_shard.at[me], dst_ref=by_shard.at[slot],
            send_sem=ssend_sems.at[peer], recv_sem=srecv_sems.at[slot],
            device_id=(g, peer), device_id_type=MESH,
        )

    def to_whole(peer, slot):
        return pltpu.make_async_remote_copy(
            src_ref=whole.at[g], dst_ref=whole.at[slot],
            send_sem=wsend_sems.at[peer], recv_sem=wrecv_sems.at[slot],
            device_id=(peer, me), device_id_type=MESH,
        )

    by_group[g] = local[g]

    pl.semaphore_wait(barrier, n - 1 + groups - 1)
    send(first).start()

    @pl.loop(1, groups)
    def _(k):
        to_group(lax.rem(g + k, groups), g).start()

    arrange(across(1), placed, across(1))
    send(across(1)).start()

    @pl.loop(1, groups)
    def _(k):
        peer = lax.rem(g + k, groups)
        to_group(peer, peer).wait_recv()

    by_shard[me] = jnp.sum(by_group[...], axis=0)

    @pl.loop(1, n)
    def _(k):
        to_shard(lax.rem(me + k, n), me).start()

    @pl.loop(2, half)
    def _(k):
        arrange(across(k), placed, across(k))
        send(across(k)).start()

    @pl.loop(1, half)
    def _(k):
        arrange(beside(k), placed, beside(k))
        send(beside(k)).start()

    index = lax.broadcasted_iota(jnp.int32, (width, width // 8), 0)
    byte = lax.broadcasted_iota(jnp.int32, (width, width // 8), 1)
    power = lax.shift_left(jnp.ones_like(index), index & 7)
    weights[...] = jnp.where(lax.shift_right_logical(index, 3) == byte, power, 0).astype(
        jnp.float32).astype(jnp.bfloat16)
    loads[2].wait()
    loads[3].wait()
    means = means_ref[...]
    inverse = 1.0 / scales_ref[...]
    step = 32 if rows % 32 == 0 else 16

    def write(source):
        at = pl.ds(pl.multiple_of(source * rows, rows), rows)
        return (
            pltpu.make_async_copy(codes.at[source], codes_hbm.at[at], codes_sems.at[source]),
            pltpu.make_async_copy(quant.at[source], quant_hbm.at[at], quant_sems.at[source]),
        )

    def encode(source):
        for r in range(0, rows, step):
            x = arrived[source, r:r + step, :].astype(jnp.float32)
            live = x < BOUND
            centered = x - means
            bits = jnp.where(live & (centered > 0), 1.0, 0.0).astype(jnp.bfloat16)
            scaled = jnp.clip(centered * inverse, -127.0, 127.0)
            quant[source, r:r + step, :] = jnp.where(live, scaled, 0.0).astype(jnp.bfloat16)
            packed = jnp.dot(bits, weights[...], preferred_element_type=jnp.float32)
            codes[source, r:r + step, :] = packed.astype(jnp.int32)
        for copy in write(source):
            copy.start()

    arrange(me, arrived, me)
    encode(me)

    @pl.loop(1, half)
    def _(k):
        receive(beside(k)).wait_recv()
        encode(beside(k))

    @pl.loop(1, n)
    def _(k):
        peer = lax.rem(me + k, n)
        to_shard(peer, peer).wait_recv()

    whole[g] = jnp.sum(by_shard[...], axis=0)

    @pl.loop(1, groups)
    def _(k):
        to_whole(lax.rem(g + k, groups), g).start()

    @pl.loop(0, half)
    def _(k):
        receive(across(k)).wait_recv()
        encode(across(k))

    @pl.loop(1, groups)
    def _(k):
        peer = lax.rem(g + k, groups)
        to_whole(peer, peer).wait_recv()

    for q in range(groups):
        stats_ref[:, q * part:(q + 1) * part] = whole[q]
    stats_write = pltpu.make_async_copy(stats_ref, stats_hbm, stats_sem)
    stats_write.start()

    @pl.loop(1, groups)
    def _(k):
        peer = lax.rem(g + k, groups)
        to_group(peer, g).wait_send()
        to_whole(peer, g).wait_send()

    @pl.loop(1, n)
    def _(k):
        peer = lax.rem(me + k, n)
        send(peer).wait_send()
        to_shard(peer, me).wait_send()

    @pl.loop(0, n)
    def _(k):
        for copy in write(k):
            copy.wait()

    stats_write.wait()


def body(n, groups, embeddings, destinations, means, scales):
    rows_in, width = embeddings.shape
    blocks = rows_in // BLOCK_ROWS
    cap = max(2, 3 * blocks // (2 * n))
    rows = cap * BLOCK_ROWS
    anywhere = pl.BlockSpec(memory_space=pl.ANY)
    dma = pltpu.SemaphoreType.DMA
    part = width // groups
    shapes = (
        jax.ShapeDtypeStruct((n * rows, width // 8), jnp.int32),
        jax.ShapeDtypeStruct((n * rows, width), jnp.bfloat16),
        jax.ShapeDtypeStruct((2, width), jnp.float32),
    )
    results = pl.pallas_call(
        functools.partial(kernel, n, groups, cap),
        out_shape=shapes,
        in_specs=[anywhere] * 4,
        out_specs=(anywhere,) * 3,
        scratch_shapes=[
            pltpu.VMEM((rows_in, width), jnp.bfloat16),
            pltpu.VMEM((1, blocks), jnp.int32),
            pltpu.VMEM((1, width), jnp.float32),
            pltpu.VMEM((1, width), jnp.float32),
            pltpu.VMEM((n, rows, width), jnp.bfloat16),
            pltpu.VMEM((n, rows, width), jnp.bfloat16),
            pltpu.VMEM((n, rows, width // 8), jnp.int32),
            pltpu.VMEM((n, rows, width), jnp.bfloat16),
            pltpu.VMEM((width, width // 8), jnp.bfloat16),
            pltpu.VMEM((groups, 2, part), jnp.float32),
            pltpu.VMEM((groups, 2, part), jnp.float32),
            pltpu.VMEM((n, 2, part), jnp.float32),
            pltpu.VMEM((groups, 2, part), jnp.float32),
            pltpu.VMEM((2, width), jnp.float32),
            dma((4,)),
            dma((n,)), dma((n,)),
            dma((groups,)), dma((groups,)),
            dma((n,)), dma((n,)),
            dma((groups,)), dma((groups,)),
            dma((n,)), dma((n,)),
            dma(()),
        ],
        compiler_params=pltpu.CompilerParams(
            collective_id=0, has_side_effects=True, vmem_limit_bytes=40 * 2**20
        ),
    )(
        embeddings, destinations.reshape(1, blocks),
        means.reshape(1, width), scales.reshape(1, width),
    )
    return results


def solution(mesh):
    n, groups = mesh.shape["shard"], mesh.shape["group"]
    in_specs = (P(("group", "shard"), None), P(("group", "shard"), None), P(), P())
    out_specs = (P(("group", "shard"), None), P(("group", "shard"), None), P())
    return jax.shard_map(
        functools.partial(body, n, groups),
        mesh=mesh, in_specs=in_specs, out_specs=out_specs, check_vma=False,
    )
```

```python
import functools

import jax
import jax.numpy as jnp
from jax import lax
from jax.experimental import pallas as pl
from jax.experimental.pallas import tpu as pltpu
from jax.sharding import PartitionSpec as P

BLOCK_ROWS = 8
ABSENT = 1024.0
BOUND = 64.0
MESH = pl.DeviceIdType.MESH


def kernel(
    n, groups, cap,
    emb_hbm, dest_hbm, means_hbm, scales_hbm,
    codes_hbm, quant_hbm, stats_hbm,
    emb, dest_ref, means_ref, scales_ref, placed, arrived, codes, quant, weights,
    local, by_group, by_shard, whole, stats_ref,
    in_sems, send_sems, recv_sems, gsend_sems, grecv_sems, ssend_sems, srecv_sems,
    wsend_sems, wrecv_sems, codes_sems, quant_sems, stats_sem,
):
    g, me = lax.axis_index("group"), lax.axis_index("shard")
    rows_in, width = emb.shape
    blocks = rows_in // BLOCK_ROWS
    rows = cap * BLOCK_ROWS
    half = n // 2
    side = me // half

    loads = [
        pltpu.make_async_copy(source, target, in_sems.at[i])
        for i, (source, target) in enumerate(
            ((dest_hbm, dest_ref), (emb_hbm, emb), (means_hbm, means_ref), (scales_hbm, scales_ref))
        )
    ]
    for load in loads:
        load.start()
    barrier = pltpu.get_barrier_semaphore()

    @pl.loop(1, n)
    def _(k):
        pl.semaphore_signal(barrier, 1, device_id=(g, lax.rem(me + k, n)), device_id_type=MESH)

    @pl.loop(1, groups)
    def _(k):
        pl.semaphore_signal(barrier, 1, device_id=(lax.rem(g + k, groups), me), device_id_type=MESH)

    loads[0].wait()
    square_block = lax.broadcasted_iota(jnp.int32, (blocks, blocks), 0)
    square_column = lax.broadcasted_iota(jnp.int32, (blocks, blocks), 1)
    owner_lanes = jnp.broadcast_to(dest_ref[...], (blocks, blocks))
    owner = jnp.sum(
        jnp.where(square_block == square_column, owner_lanes, 0), axis=1, keepdims=True
    )
    block = lax.broadcasted_iota(jnp.int32, (blocks, rows_in), 0)
    column = lax.broadcasted_iota(jnp.int32, (blocks, rows_in), 1)
    column_block = lax.shift_right_logical(column, BLOCK_ROWS.bit_length() - 1)
    owner_wide = jnp.broadcast_to(owner, (blocks, rows_in))
    owner_row = jnp.sum(jnp.where(block == column_block, owner_wide, 0), axis=0, keepdims=True)
    before = (owner_wide == owner_row) & (block < column_block)
    slot_row = jnp.sum(before.astype(jnp.int32), axis=0, keepdims=True)
    target_row = (owner_row * cap + slot_row) * BLOCK_ROWS + (column[:1] & (BLOCK_ROWS - 1))
    place = lax.broadcasted_iota(jnp.int32, (rows, rows_in), 0)
    place_row = lax.broadcasted_iota(jnp.int32, (rows, width), 0)

    def arrange(peer, out, at):
        picks = (target_row - peer * rows == place).astype(jnp.float32).astype(jnp.bfloat16)
        count = jnp.sum((owner == peer).astype(jnp.int32), axis=0, keepdims=True)
        moved = jnp.dot(picks, emb[...], preferred_element_type=jnp.float32)
        filled = place_row < jnp.broadcast_to(count * BLOCK_ROWS, (rows, width))
        out[at] = jnp.where(filled, moved, ABSENT).astype(jnp.bfloat16)

    def across(k):
        return (1 - side) * half + (lax.rem(me, half) ^ k if half & (half - 1) == 0 else lax.rem(me + k, half))

    def beside(k):
        return side * half + lax.rem(me + k, half)

    def send(peer):
        return pltpu.make_async_remote_copy(
            src_ref=placed.at[peer], dst_ref=arrived.at[me],
            send_sem=send_sems.at[peer], recv_sem=recv_sems.at[me],
            device_id=(g, peer), device_id_type=MESH,
        )

    def receive(peer):
        return pltpu.make_async_remote_copy(
            src_ref=placed.at[peer], dst_ref=arrived.at[peer],
            send_sem=send_sems.at[peer], recv_sem=recv_sems.at[peer],
            device_id=(g, peer), device_id_type=MESH,
        )

    loads[1].wait()
    first = across(0)
    arrange(first, placed, first)
    tile = 64
    total = jnp.zeros((8, width), jnp.float32)
    square = jnp.zeros((8, width), jnp.float32)

    def add(i, carry):
        total, square = carry
        x = emb[pl.ds(pl.multiple_of(i * tile, tile), tile), :].astype(jnp.float32)
        x = x.reshape(tile // 8, 8, width)
        return total + jnp.sum(x, axis=0), square + jnp.sum(x * x, axis=0)

    total, square = lax.fori_loop(0, rows_in // tile, add, (total, square))
    part = width // groups
    total = jnp.sum(total, axis=0, keepdims=True)
    square = jnp.sum(square, axis=0, keepdims=True)
    for q in range(groups):
        local[q, 0:1, :] = total[:, q * part:(q + 1) * part]
        local[q, 1:2, :] = square[:, q * part:(q + 1) * part]

    def to_group(peer, slot):
        return pltpu.make_async_remote_copy(
            src_ref=local.at[peer], dst_ref=by_group.at[slot],
            send_sem=gsend_sems.at[peer], recv_sem=grecv_sems.at[slot],
            device_id=(peer, me), device_id_type=MESH,
        )

    def to_shard(peer, slot):
        return pltpu.make_async_remote_copy(
            src_ref=by_shard.at[me], dst_ref=by_shard.at[slot],
            send_sem=ssend_sems.at[peer], recv_sem=srecv_sems.at[slot],
            device_id=(g, peer), device_id_type=MESH,
        )

    def to_whole(peer, slot):
        return pltpu.make_async_remote_copy(
            src_ref=whole.at[g], dst_ref=whole.at[slot],
            send_sem=wsend_sems.at[peer], recv_sem=wrecv_sems.at[slot],
            device_id=(peer, me), device_id_type=MESH,
        )

    by_group[g] = local[g]

    pl.semaphore_wait(barrier, n - 1 + groups - 1)
    send(first).start()

    @pl.loop(1, groups)
    def _(k):
        to_group(lax.rem(g + k, groups), g).start()

    arrange(across(1), placed, across(1))
    send(across(1)).start()

    @pl.loop(1, groups)
    def _(k):
        peer = lax.rem(g + k, groups)
        to_group(peer, peer).wait_recv()

    by_shard[me] = jnp.sum(by_group[...], axis=0)

    @pl.loop(1, n)
    def _(k):
        to_shard(lax.rem(me + k, n), me).start()

    @pl.loop(2, half)
    def _(k):
        arrange(across(k), placed, across(k))
        send(across(k)).start()

    @pl.loop(1, half)
    def _(k):
        arrange(beside(k), placed, beside(k))
        send(beside(k)).start()

    index = lax.broadcasted_iota(jnp.int32, (width, width // 8), 0)
    byte = lax.broadcasted_iota(jnp.int32, (width, width // 8), 1)
    power = lax.shift_left(jnp.ones_like(index), index & 7)
    weights[...] = jnp.where(lax.shift_right_logical(index, 3) == byte, power, 0).astype(
        jnp.float32).astype(jnp.bfloat16)
    loads[2].wait()
    loads[3].wait()
    means = means_ref[...]
    inverse = 1.0 / scales_ref[...]
    step = 32 if rows % 32 == 0 else 16

    def write(source):
        at = pl.ds(pl.multiple_of(source * rows, rows), rows)
        return (
            pltpu.make_async_copy(codes.at[source], codes_hbm.at[at], codes_sems.at[source]),
            pltpu.make_async_copy(quant.at[source], quant_hbm.at[at], quant_sems.at[source]),
        )

    def encode(source):
        for r in range(0, rows, step):
            x = arrived[source, r:r + step, :].astype(jnp.float32)
            live = x < BOUND
            centered = x - means
            bits = jnp.where(live & (centered > 0), 1.0, 0.0).astype(jnp.bfloat16)
            scaled = jnp.clip(centered * inverse, -127.0, 127.0)
            quant[source, r:r + step, :] = jnp.where(live, scaled, 0.0).astype(jnp.bfloat16)
            packed = jnp.dot(bits, weights[...], preferred_element_type=jnp.float32)
            codes[source, r:r + step, :] = packed.astype(jnp.int32)
        for copy in write(source):
            copy.start()

    arrange(me, arrived, me)
    encode(me)

    @pl.loop(1, half)
    def _(k):
        receive(beside(k)).wait_recv()
        encode(beside(k))

    @pl.loop(1, n)
    def _(k):
        peer = lax.rem(me + k, n)
        to_shard(peer, peer).wait_recv()

    whole[g] = jnp.sum(by_shard[...], axis=0)

    @pl.loop(1, groups)
    def _(k):
        to_whole(lax.rem(g + k, groups), g).start()

    @pl.loop(0, half)
    def _(k):
        receive(across(k)).wait_recv()
        encode(across(k))

    @pl.loop(1, groups)
    def _(k):
        peer = lax.rem(g + k, groups)
        to_whole(peer, peer).wait_recv()

    for q in range(groups):
        stats_ref[:, q * part:(q + 1) * part] = whole[q]
    stats_write = pltpu.make_async_copy(stats_ref, stats_hbm, stats_sem)
    stats_write.start()

    @pl.loop(1, groups)
    def _(k):
        peer = lax.rem(g + k, groups)
        to_group(peer, g).wait_send()
        to_whole(peer, g).wait_send()

    @pl.loop(1, n)
    def _(k):
        peer = lax.rem(me + k, n)
        send(peer).wait_send()
        to_shard(peer, me).wait_send()

    @pl.loop(0, n)
    def _(k):
        for copy in write(k):
            copy.wait()

    stats_write.wait()


def hand_over(
    n, codes_in, quant_in, stats_in, codes_out, quant_out, stats_out,
    codes, quant, stats, codes_load, quant_load, codes_store, quant_store, stats_sems,
):
    rows = codes.shape[0] // n

    def steps(k):
        at = pl.ds(pl.multiple_of(k * rows, rows), rows)
        return (
            pltpu.make_async_copy(quant_in.at[at], quant.at[at], quant_load.at[k]),
            pltpu.make_async_copy(codes_in.at[at], codes.at[at], codes_load.at[k]),
            pltpu.make_async_copy(quant.at[at], quant_out.at[at], quant_store.at[k]),
            pltpu.make_async_copy(codes.at[at], codes_out.at[at], codes_store.at[k]),
        )

    stats_load = pltpu.make_async_copy(stats_in, stats, stats_sems.at[0])
    stats_store = pltpu.make_async_copy(stats, stats_out, stats_sems.at[1])
    stats_load.start()

    @pl.loop(0, n)
    def _(k):
        for copy in steps(k)[:2]:
            copy.start()

    stats_load.wait()
    stats_store.start()

    @pl.loop(0, n)
    def _(k):
        load_quant, load_codes, store_quant, store_codes = steps(k)
        load_quant.wait()
        store_quant.start()
        load_codes.wait()
        store_codes.start()

    stats_store.wait()

    @pl.loop(0, n)
    def _(k):
        for copy in steps(k)[2:]:
            copy.wait()


def body(n, groups, embeddings, destinations, means, scales):
    rows_in, width = embeddings.shape
    blocks = rows_in // BLOCK_ROWS
    cap = max(2, 3 * blocks // (2 * n))
    rows = cap * BLOCK_ROWS
    anywhere = pl.BlockSpec(memory_space=pl.ANY)
    dma = pltpu.SemaphoreType.DMA
    part = width // groups
    shapes = (
        jax.ShapeDtypeStruct((n * rows, width // 8), jnp.int32),
        jax.ShapeDtypeStruct((n * rows, width), jnp.bfloat16),
        jax.ShapeDtypeStruct((2, width), jnp.float32),
    )
    results = pl.pallas_call(
        functools.partial(kernel, n, groups, cap),
        out_shape=shapes,
        in_specs=[anywhere] * 4,
        out_specs=(anywhere,) * 3,
        scratch_shapes=[
            pltpu.VMEM((rows_in, width), jnp.bfloat16),
            pltpu.VMEM((1, blocks), jnp.int32),
            pltpu.VMEM((1, width), jnp.float32),
            pltpu.VMEM((1, width), jnp.float32),
            pltpu.VMEM((n, rows, width), jnp.bfloat16),
            pltpu.VMEM((n, rows, width), jnp.bfloat16),
            pltpu.VMEM((n, rows, width // 8), jnp.int32),
            pltpu.VMEM((n, rows, width), jnp.bfloat16),
            pltpu.VMEM((width, width // 8), jnp.bfloat16),
            pltpu.VMEM((groups, 2, part), jnp.float32),
            pltpu.VMEM((groups, 2, part), jnp.float32),
            pltpu.VMEM((n, 2, part), jnp.float32),
            pltpu.VMEM((groups, 2, part), jnp.float32),
            pltpu.VMEM((2, width), jnp.float32),
            dma((4,)),
            dma((n,)), dma((n,)),
            dma((groups,)), dma((groups,)),
            dma((n,)), dma((n,)),
            dma((groups,)), dma((groups,)),
            dma((n,)), dma((n,)),
            dma(()),
        ],
        compiler_params=pltpu.CompilerParams(
            collective_id=0, has_side_effects=True, vmem_limit_bytes=58 * 2**20
        ),
    )(
        embeddings, destinations.reshape(1, blocks),
        means.reshape(1, width), scales.reshape(1, width),
    )
    return pl.pallas_call(
        functools.partial(hand_over, n),
        out_shape=shapes,
        in_specs=[anywhere] * 3,
        out_specs=(anywhere,) * 3,
        scratch_shapes=[pltpu.VMEM(shape.shape, shape.dtype) for shape in shapes]
        + [dma((n,))] * 4 + [dma((2,))],
        compiler_params=pltpu.CompilerParams(vmem_limit_bytes=58 * 2**20),
    )(*results)


def solution(mesh):
    n, groups = mesh.shape["shard"], mesh.shape["group"]
    in_specs = (P(("group", "shard"), None), P(("group", "shard"), None), P(), P())
    out_specs = (P(("group", "shard"), None), P(("group", "shard"), None), P())
    return jax.shard_map(
        functools.partial(body, n, groups),
        mesh=mesh, in_specs=in_specs, out_specs=out_specs, check_vma=False,
    )
```
